512 devices in a mesh: fsdp: 32 (over x, y, core), tx: 4 (over z_hi), ty: 4 (over z_lo).
Axes of the slice: x: 4, y: 4, z: 16 (z_hi: 4, z_lo: 4; z = z_hi * 4 + z_lo), core: 2. Of those that a mesh axis runs over, the one named last changes fastest.
Arguments:
- context: bfloat16 [32768, 4096], P('fsdp', ('tx', 'ty')), may hold values from -6 to 6
- residual: bfloat16 [32768, 8192], P('fsdp', ('ty', 'tx')), may hold values from -30 to 30
- policy_weight: bfloat16 [8192, 4096], P(('ty', 'fsdp'), 'tx'), may hold values from -0.09375 to 0.09375
- master_weight: float32 [8192, 4096], P(('ty', 'fsdp'), 'tx'), may hold values from -0.09375 to 0.09375
- norm_gain: bfloat16 [8192], P(('ty', 'tx')), may hold values from 0.099609375 to 1.8984375
Outputs:
- normed: bfloat16 [32768, 8192], P('fsdp', ('ty', 'tx'))
- new_master: float32 [8192, 4096], P(('ty', 'fsdp'), 'tx')
The draws below stay inside these ranges and needn't reach their ends.
All inputs are finite; a program needn't handle non-finite values.
Results may differ from the reference program's by a relative error of at most 0.013.
Values may be sent and summed in bfloat16 or wider, within the bound.
No kernel may reach another device: no remote copies, remote signals or barrier semaphores. Data moves between devices by JAX's collectives and lax.ppermute only.
A program may use at most 64 MiB of HBM per device.

```python
import math
import jax
import jax.numpy as jnp
from jax import lax

D = 8192
H = 4096
TOKENS = 32768
N_TX = 4


def draw_residual(key, part):
    key = jax.random.fold_in(key, 7)
    key_base, key_rows, key_cols = jax.random.split(key, 3)
    positions = jnp.arange(D, dtype=jnp.float32) / D
    column_scale = jnp.exp(positions * math.log(3.0) + jax.random.uniform(key_cols, (D,), jnp.float32, -0.5, 0.5))
    row_scale = jnp.exp(jax.random.uniform(key_rows, (TOKENS, 1), jnp.float32, math.log(0.3), math.log(3.0)))
    base_values = jnp.clip(jax.random.normal(key_base, (TOKENS, D), jnp.float32), -4.0, 4.0)
    return (0.5 * base_values * row_scale * column_scale[None, :]).astype(jnp.bfloat16)


def levels(key, extent, pieces, low, top_value):
    gain = 1.0
    for position, parts in pieces:
        steps = jax.random.uniform(jax.random.fold_in(jax.random.fold_in(key, 6), position), (parts,), jnp.float32, low / len(pieces), top_value / len(pieces))
        gain = gain * jnp.repeat(jnp.exp(steps), extent[position] // parts).reshape((-1,) + (1,) * (len(extent) - 1 - position))
    return gain


def normal_values(rng, dims, spread, bound, cuts=(), kind=jnp.bfloat16):
    factor_of = levels(rng, dims, cuts, -0.22, 0.18) if cuts else 1.0
    result = jax.random.normal(rng, dims, jnp.float32) * spread * factor_of
    return jnp.minimum(jnp.maximum(result, -bound), bound).astype(kind)


def setup_inputs(seed: int = 0) -> dict:
    key_of = jax.random.split(jax.random.key(seed), 6)
    context = normal_values(key_of[0], (TOKENS, H), 1.0, 6.0, ((0, 32), (1, 16)))
    residual = draw_residual(jax.random.fold_in(key_of[5], 71), 0)
    policy_weight = normal_values(key_of[2], (D, H), H ** -0.5, 0.09375, ((0, 128), (1, 4)))
    master_weight = normal_values(key_of[3], (D, H), H ** -0.5, 0.09375, ((0, 128), (1, 4)), jnp.float32)
    norm_gain = jnp.clip(1.0 + 0.18 * jax.random.normal(key_of[4], (D,), jnp.float32), 0.099609375, 1.8984375).astype(jnp.bfloat16)
    return {"context": context, "residual": residual, "policy_weight": policy_weight, "master_weight": master_weight, "norm_gain": norm_gain}


mix_rate = 0.6

def reference(context, residual, policy_weight, master_weight, norm_gain):
    new_master = mix_rate * policy_weight.astype(jnp.float32) + (1.0 - mix_rate) * master_weight
    recast_weight = new_master.astype(jnp.bfloat16)
    column_block = H // N_TX
    hidden = residual.astype(jnp.float32)
    for block_index in range(N_TX):
        first = block_index * column_block
        context_part = context[:, first:first + column_block]
        weight_part = recast_weight[:, first:first + column_block]
        partial_value = lax.dot_general(context_part, weight_part, (((1,), (1,)), ((), ())), preferred_element_type=jnp.float32)
        rounded = lax.optimization_barrier(partial_value.astype(jnp.bfloat16))
        hidden = hidden + rounded.astype(jnp.float32)
    square_mean = lax.optimization_barrier(jnp.mean(hidden * hidden, axis=1, keepdims=True))
    normed = (hidden * lax.rsqrt(square_mean + 1e-05) * norm_gain.astype(jnp.float32)).astype(jnp.bfloat16)
    return (normed, new_master)
```

```python
import functools

import jax
import jax.numpy as jnp
from jax import lax
from jax.experimental import pallas as pl
from jax.experimental.pallas import tpu as pltpu
from jax.sharding import PartitionSpec as P

D = 8192
Z = ("tx", "ty")
NZ = 16

mix_rate = 0.6

TOK = 1024
FEAT = 256
COLS = 512
TILE = 256

UP = [(i, (i + 1) % NZ) for i in range(NZ)]
DOWN = [(i, (i - 1) % NZ) for i in range(NZ)]

SPREAD = []
LIFT = []
for u in range(4):
    for r in range(8):
        for t in range(4):
            s = (u - t) % 4
            SPREAD.append(((8 * u + r) * 4 + t, (4 * r + s) * 4 + t))
            LIFT.append(((4 * r + s) * 4 + t, (4 * r + s) * 4 + u))


def product_kernel(shifts, squares, z_ref, base_ref, weight_ref, *refs):
    blocks = refs[: len(shifts)]
    outs = refs[len(shifts) :]
    z = z_ref[0]
    total = base_ref[...].astype(jnp.float32)
    for shift, block in zip(shifts, blocks):
        source = lax.rem(z + (shift % NZ), NZ)
        turn = lax.rem(z // 4 - source // 4 + 4, 4)
        offset = pl.multiple_of(lax.rem(source, 4) * FEAT, FEAT)
        weight = weight_ref[:, turn, :, pl.ds(offset, FEAT)].reshape(COLS, FEAT)
        total += lax.dot_general(
            block[...], weight, (((1,), (1,)), ((), ())), preferred_element_type=jnp.float32
        )
    outs[0][...] = total
    if squares:
        ones = jnp.ones((8, COLS), jnp.float32)
        outs[1][...] = lax.dot_general(
            ones,
            total * total,
            (((1,), (1,)), ((), ())),
            precision=lax.Precision.HIGHEST,
            preferred_element_type=jnp.float32,
        )


def product(z, base, weight, shifts, blocks, squares):
    n = TOK // TILE
    whole = pl.BlockSpec((8, 4, 64, 1024), lambda i, z: (0, 0, 0, 0))
    out_shape = [jax.ShapeDtypeStruct((TOK, COLS), jnp.float32)]
    out_specs = [pl.BlockSpec((TILE, COLS), lambda i, z: (i, 0))]
    if squares:
        out_shape.append(jax.ShapeDtypeStruct((8, TOK), jnp.float32))
        out_specs.append(pl.BlockSpec((8, TILE), lambda i, z: (0, i)))
    return pl.pallas_call(
        functools.partial(product_kernel, shifts, squares),
        out_shape=out_shape,
        grid_spec=pltpu.PrefetchScalarGridSpec(
            num_scalar_prefetch=1,
            grid=(n,),
            in_specs=[pl.BlockSpec((TILE, COLS), lambda i, z: (i, 0)), whole]
            + [pl.BlockSpec((TILE, FEAT), lambda i, z: (i, 0))] * len(blocks),
            out_specs=out_specs,
        ),
        compiler_params=pltpu.CompilerParams(vmem_limit_bytes=40 * 1024 * 1024),
        cost_estimate=pl.CostEstimate(
            flops=2 * TOK * COLS * FEAT * len(blocks),
            bytes_accessed=4 * 1024 * 1024 + len(blocks) * TOK * FEAT * 2 + TOK * COLS * 8,
            transcendentals=0,
        ),
    )(z, base, weight, *blocks)


def shards(context, residual, policy_weight, master_weight, norm_gain):
    new_master = mix_rate * policy_weight.astype(jnp.float32) + (1.0 - mix_rate) * master_weight
    recast = new_master.astype(jnp.bfloat16)
    spread = lax.ppermute(recast, ("fsdp", "tx"), SPREAD)
    lifted = lax.ppermute(spread, ("fsdp", "tx"), LIFT)
    weight = lax.all_gather(lifted, "fsdp", axis=0).reshape(8, 4, 64, 1024)

    z = (lax.axis_index("tx") * 4 + lax.axis_index("ty")).astype(jnp.int32).reshape(1)
    below = above = context
    shifts, blocks = [0], [context]
    for step in range(1, 8):
        below = lax.ppermute(below, Z, UP)
        above = lax.ppermute(above, Z, DOWN)
        shifts += [-step, step]
        blocks += [below, above]
    half = TOK // 2
    far_low = lax.ppermute(below[:half], Z, UP)
    far_high = lax.ppermute(above[half:], Z, DOWN)
    far = jnp.concatenate([far_low, far_high], axis=0)

    (partial,) = product(z, residual, weight, shifts[:13], blocks[:13], False)
    hidden, squares = product(z, partial, weight, shifts[13:] + [8], blocks[13:] + [far], True)

    sent = jnp.broadcast_to(squares[:1], (NZ, TOK))
    totals = jnp.sum(lax.all_to_all(sent, Z, 0, 0, tiled=True), axis=0)
    square_mean = (totals / D)[:, None]
    normed = (
        hidden * lax.rsqrt(square_mean + 1e-05) * norm_gain.astype(jnp.float32)[None, :]
    ).astype(jnp.bfloat16)
    return (normed, new_master)


def solution(mesh):
    return jax.shard_map(
        shards,
        mesh=mesh,
        in_specs=(
            P("fsdp", ("tx", "ty")),
            P("fsdp", ("ty", "tx")),
            P(("ty", "fsdp"), "tx"),
            P(("ty", "fsdp"), "tx"),
            P(("ty", "tx")),
        ),
        out_specs=(P("fsdp", ("ty", "tx")), P(("ty", "fsdp"), "tx")),
        check_vma=False,
    )
```

```python
import jax
import jax.numpy as jnp
from jax import lax
from jax.experimental import pallas as pl
from jax.experimental.pallas import tpu as pltpu
from jax.sharding import PartitionSpec as P

D = 8192
H = 4096
Z = ("tx", "ty")
ALL = ("fsdp", "tx", "ty")
NZ = 16

mix_rate = 0.6

TOK = 1024
FEAT = 256
COLS = 512
TILE = 256


def place(f, t, y):
    return (f * 4 + t) * 4 + y


def column(r, turn):
    return ((r % 4) * 4 + (turn % 2) * 2 + r // 4) * 2 + turn // 2


SPREAD = []
for y in range(4):
    for u in range(4):
        for r in range(8):
            for t in range(4):
                SPREAD.append((place(8 * u + r, t, y), place(column(r, (u - t + y) % 4), u, y)))


def partner(dx, dy, dc):
    pairs = []
    for x in range(4):
        for y in range(4):
            for c in range(2):
                pairs.append(((x * 4 + y) * 2 + c, ((x ^ dx) * 4 + (y ^ dy)) * 2 + (c ^ dc)))
    return pairs


def kernel(z_ref, base_ref, weight_ref, context_ref, out_ref, squares_ref):
    part = pl.program_id(0)
    first = z_ref[0] // 4 + z_ref[0] % 4
    block = jnp.concatenate(
        [context_ref[(first - turn + 4) % 4 * 4 + i] for turn in range(4) for i in range(4)],
        axis=1,
    )
    total = base_ref[...].astype(jnp.float32) + jnp.dot(
        block, weight_ref[...], preferred_element_type=jnp.float32
    )
    out_ref[...] = total
    squared = total * total
    lanes = sum(squared[:, i * 128 : (i + 1) * 128] for i in range(COLS // 128))
    sums = jnp.sum(lanes.T, axis=0, keepdims=True)
    for i in range(TILE // 128):
        squares_ref[:, pl.ds(part * (TILE // 128) + i, 1), :] = jnp.broadcast_to(
            sums[:, i * 128 : (i + 1) * 128][None], (NZ, 1, 128)
        )


def product(z, base, weight, context):
    row = lambda i, z: (i, 0)
    return pl.pallas_call(
        kernel,
        out_shape=[
            jax.ShapeDtypeStruct((TOK, COLS), jnp.float32),
            jax.ShapeDtypeStruct((NZ, TOK // 128, 128), jnp.float32),
        ],
        grid_spec=pltpu.PrefetchScalarGridSpec(
            num_scalar_prefetch=1,
            grid=(TOK // TILE,),
            in_specs=[
                pl.BlockSpec((TILE, COLS), row),
                pl.BlockSpec((H, COLS), lambda i, z: (0, 0)),
                pl.BlockSpec((NZ, TILE, FEAT), lambda i, z: (0, i, 0)),
            ],
            out_specs=[
                pl.BlockSpec((TILE, COLS), row),
                pl.BlockSpec((NZ, TOK // 128, 128), lambda i, z: (0, 0, 0)),
            ],
        ),
        compiler_params=pltpu.CompilerParams(vmem_limit_bytes=58 * 1024 * 1024),
        cost_estimate=pl.CostEstimate(
            flops=2 * TOK * COLS * H,
            bytes_accessed=(TOK + COLS) * H * 2 + TOK * COLS * 6,
            transcendentals=0,
        ),
    )(z, base, weight, context)


def shards(context, residual, policy_weight, master_weight, norm_gain):
    new_master = mix_rate * policy_weight.astype(jnp.float32) + (1.0 - mix_rate) * master_weight
    recast = new_master.astype(jnp.bfloat16)

    z = (lax.axis_index("tx") * 4 + lax.axis_index("ty")).astype(jnp.int32)
    f = lax.axis_index("fsdp")
    x, y, c = f // 8, (f // 2) % 4, f % 2

    gathered = lax.all_gather(context, Z, axis=0)
    piece = lax.ppermute(recast, ALL, SPREAD)

    row = jnp.zeros((4, 64, 1024), jnp.bfloat16)
    for dx in range(4):
        got = piece if dx == 0 else lax.ppermute(piece, "fsdp", partner(dx, 0, 0))
        row = lax.dynamic_update_slice(row, got[None], (x ^ dx, 0, 0))
    near = lax.ppermute(row, "fsdp", partner(0, 1, 0))
    back = lax.ppermute(row, "fsdp", partner(0, 3, 0))
    low = lax.ppermute(back[:2], "fsdp", partner(0, 1, 0))
    high = lax.ppermute(near[2:], "fsdp", partner(0, 3, 0))
    plane = jnp.zeros((16, 64, 1024), jnp.bfloat16)
    for got, dy, at in ((row, 0, 0), (near, 1, 0), (back, 3, 0), (low, 2, 0), (high, 2, 2)):
        plane = lax.dynamic_update_slice(plane, got, ((y ^ dy) * 4 + at, 0, 0))
    other = lax.ppermute(plane, "fsdp", partner(0, 0, 1))
    pieces = jnp.zeros((32, 64, 1024), jnp.bfloat16)
    pieces = lax.dynamic_update_slice(pieces, plane, (c * 16, 0, 0))
    pieces = lax.dynamic_update_slice(pieces, other, ((1 - c) * 16, 0, 0))
    weight = pieces.reshape(4, COLS, 1024).transpose(0, 2, 1).reshape(H, COLS)
    hidden, squares = product(z[None], residual, weight, gathered)

    totals = jnp.sum(lax.all_to_all(squares, Z, 0, 0, tiled=True), axis=0)
    square_mean = (totals.reshape(TOK) / D)[:, None]
    normed = (
        hidden * lax.rsqrt(square_mean + 1e-05) * norm_gain.astype(jnp.float32)[None, :]
    ).astype(jnp.bfloat16)
    return (normed, new_master)


def solution(mesh):
    return jax.shard_map(
        shards,
        mesh=mesh,
        in_specs=(
            P("fsdp", ("tx", "ty")),
            P("fsdp", ("ty", "tx")),
            P(("ty", "fsdp"), "tx"),
            P(("ty", "fsdp"), "tx"),
            P(("ty", "tx")),
        ),
        out_specs=(P("fsdp", ("ty", "tx")), P(("ty", "fsdp"), "tx")),
        check_vma=False,
    )
```

```python
import jax
import jax.numpy as jnp
from jax import lax
from jax.experimental import pallas as pl
from jax.experimental.pallas import tpu as pltpu
from jax.sharding import PartitionSpec as P

D = 8192
H = 4096
Z = ("tx", "ty")
ALL = ("fsdp", "tx", "ty")
NZ = 16

mix_rate = 0.6

TOK = 1024
FEAT = 256
COLS = 512


def place(f, t, y):
    return (f * 4 + t) * 4 + y


def column(r, turn):
    return ((r % 4) * 4 + (turn % 2) * 2 + r // 4) * 2 + turn // 2


SPREAD = []
for y in range(4):
    for u in range(4):
        for r in range(8):
            for t in range(4):
                SPREAD.append((place(8 * u + r, t, y), place(column(r, (u - t + y) % 4), u, y)))


def partner(dx, dy, dc):
    pairs = []
    for x in range(4):
        for y in range(4):
            for c in range(2):
                pairs.append(((x * 4 + y) * 2 + c, ((x ^ dx) * 4 + (y ^ dy)) * 2 + (c ^ dc)))
    return pairs


def kernel(z_ref, base_hbm, weight_hbm, context_hbm, out_ref, squares_ref, base, weight, context, sems):
    first = z_ref[0] // 4 + z_ref[0] % 4
    copies = []
    for turn in range(4):
        plane = pl.ds((first - turn + 4) % 4 * 4, 4)
        copies.append(
            (
                pltpu.make_async_copy(weight_hbm.at[turn], weight.at[turn], sems.at[2 * turn]),
                pltpu.make_async_copy(
                    context_hbm.at[plane], context.at[turn], sems.at[2 * turn + 1]
                ),
            )
        )
    base_copy = pltpu.make_async_copy(base_hbm, base, sems.at[8])
    for pair in copies:
        pair[0].start()
        pair[1].start()
    base_copy.start()
    total = 0
    for turn, pair in enumerate(copies):
        pair[0].wait()
        pair[1].wait()
        block = jnp.concatenate([context[turn, i] for i in range(4)], axis=1)
        total += jnp.dot(block, weight[turn], preferred_element_type=jnp.float32)
    base_copy.wait()
    total += base[...].astype(jnp.float32)
    out_ref[...] = total.astype(jnp.bfloat16)
    squared = total * total
    lanes = sum(squared[:, i * 128 : (i + 1) * 128] for i in range(COLS // 128))
    sums = jnp.sum(lanes.T, axis=0, keepdims=True)
    for i in range(TOK // 128):
        squares_ref[:, i : i + 1, :] = jnp.broadcast_to(
            sums[:, i * 128 : (i + 1) * 128][None], (NZ, 1, 128)
        )


def product(z, base, weight, context):
    return pl.pallas_call(
        kernel,
        out_shape=[
            jax.ShapeDtypeStruct((TOK, COLS), jnp.bfloat16),
            jax.ShapeDtypeStruct((NZ, TOK // 128, 128), jnp.float32),
        ],
        in_specs=[pl.BlockSpec(memory_space=pltpu.SMEM)]
        + [pl.BlockSpec(memory_space=pltpu.HBM)] * 3,
        out_specs=[pl.BlockSpec(memory_space=pltpu.VMEM)] * 2,
        scratch_shapes=[
            pltpu.VMEM((TOK, COLS), jnp.bfloat16),
            pltpu.VMEM((4, 1024, COLS), jnp.bfloat16),
            pltpu.VMEM((4, 4, TOK, FEAT), jnp.bfloat16),
            pltpu.SemaphoreType.DMA((9,)),
        ],
        compiler_params=pltpu.CompilerParams(vmem_limit_bytes=60 * 1024 * 1024),
        cost_estimate=pl.CostEstimate(
            flops=2 * TOK * COLS * H,
            bytes_accessed=(TOK + COLS) * H * 2 + TOK * COLS * 4,
            transcendentals=0,
        ),
    )(z, base, weight, context)


def shards(context, residual, policy_weight, master_weight, norm_gain):
    new_master = mix_rate * policy_weight.astype(jnp.float32) + (1.0 - mix_rate) * master_weight
    recast = new_master.astype(jnp.bfloat16)

    z = (lax.axis_index("tx") * 4 + lax.axis_index("ty")).astype(jnp.int32)
    f = lax.axis_index("fsdp")
    x, y, c = f // 8, (f // 2) % 4, f % 2

    gathered = lax.all_gather(context, Z, axis=0)
    piece = lax.ppermute(recast, ALL, SPREAD)

    row = jnp.zeros((4, 64, 1024), jnp.bfloat16)
    for dx in range(4):
        got = piece if dx == 0 else lax.ppermute(piece, "fsdp", partner(dx, 0, 0))
        row = lax.dynamic_update_slice(row, got[None], (x ^ dx, 0, 0))
    near = lax.ppermute(row, "fsdp", partner(0, 1, 0))
    back = lax.ppermute(row, "fsdp", partner(0, 3, 0))
    low = lax.ppermute(back[:2], "fsdp", partner(0, 1, 0))
    high = lax.ppermute(near[2:], "fsdp", partner(0, 3, 0))
    plane = jnp.zeros((16, 64, 1024), jnp.bfloat16)
    for got, dy, at in ((row, 0, 0), (near, 1, 0), (back, 3, 0), (low, 2, 0), (high, 2, 2)):
        plane = lax.dynamic_update_slice(plane, got, ((y ^ dy) * 4 + at, 0, 0))
    other = lax.ppermute(plane, "fsdp", partner(0, 0, 1))
    pieces = jnp.zeros((32, 64, 1024), jnp.bfloat16)
    pieces = lax.dynamic_update_slice(pieces, plane, (c * 16, 0, 0))
    pieces = lax.dynamic_update_slice(pieces, other, ((1 - c) * 16, 0, 0))
    weight = pieces.reshape(4, COLS, 1024).transpose(0, 2, 1)
    hidden, squares = product(z[None], residual, weight, gathered)

    totals = jnp.sum(lax.all_to_all(squares, Z, 0, 0, tiled=True), axis=0)
    square_mean = (totals.reshape(TOK) / D)[:, None]
    normed = (
        hidden * lax.rsqrt(square_mean + 1e-05) * norm_gain.astype(jnp.float32)[None, :]
    ).astype(jnp.bfloat16)
    return (normed, new_master)


def solution(mesh):
    return jax.shard_map(
        shards,
        mesh=mesh,
        in_specs=(
            P("fsdp", ("tx", "ty")),
            P("fsdp", ("ty", "tx")),
            P(("ty", "fsdp"), "tx"),
            P(("ty", "fsdp"), "tx"),
            P(("ty", "tx")),
        ),
        out_specs=(P("fsdp", ("ty", "tx")), P(("ty", "fsdp"), "tx")),
        check_vma=False,
    )
```

```python
import jax
import jax.numpy as jnp
from jax import lax
from jax.experimental import pallas as pl
from jax.experimental.pallas import tpu as pltpu
from jax.sharding import PartitionSpec as P

D = 8192
H = 4096
Z = ("tx", "ty")
ALL = ("fsdp", "tx", "ty")
NZ = 16

mix_rate = 0.6

TOK = 1024
FEAT = 256
COLS = 512


def place(f, t, y):
    return (f * 4 + t) * 4 + y


def column(r, turn):
    return ((r % 4) * 4 + (turn % 2) * 2 + r // 4) * 2 + turn // 2


SPREAD = []
LIFT = []
LIFT_ON = []
for y in range(4):
    for u in range(4):
        for r in range(8):
            for t in range(4):
                there = column(r, (u - t + y) % 4)
                SPREAD.append((place(8 * u + r, t, y), place(there, t, y)))
                step = (0, 1, 1 - 2 * (there % 2), -1)[(u - t) % 4]
                middle = (t + step) % 4
                LIFT.append((place(there, t, y), place(there, middle, y)))
                LIFT_ON.append((place(there, middle, y), place(there, u, y)))


def partner(dx, dy, dc):
    pairs = []
    for x in range(4):
        for y in range(4):
            for c in range(2):
                pairs.append(((x * 4 + y) * 2 + c, ((x ^ dx) * 4 + (y ^ dy)) * 2 + (c ^ dc)))
    return pairs


def kernel(z_ref, base_hbm, weight_hbm, context_hbm, out_ref, squares_ref, base, weight, context, sems):
    first = z_ref[0] // 4 + z_ref[0] % 4
    copies = []
    for turn in range(4):
        plane = pl.ds((first - turn + 4) % 4 * 4, 4)
        copies.append(
            (
                pltpu.make_async_copy(weight_hbm.at[turn], weight.at[turn], sems.at[2 * turn]),
                pltpu.make_async_copy(
                    context_hbm.at[plane], context.at[turn], sems.at[2 * turn + 1]
                ),
            )
        )
    base_copy = pltpu.make_async_copy(base_hbm, base, sems.at[8])
    for pair in copies:
        pair[0].start()
        pair[1].start()
    base_copy.start()
    total = 0
    for turn, pair in enumerate(copies):
        pair[0].wait()
        pair[1].wait()
        block = jnp.concatenate([context[turn, i] for i in range(4)], axis=1)
        total += jnp.dot(block, weight[turn], preferred_element_type=jnp.float32)
    base_copy.wait()
    total += base[...].astype(jnp.float32)
    out_ref[...] = total.astype(jnp.bfloat16)
    squared = total * total
    lanes = sum(squared[:, i * 128 : (i + 1) * 128] for i in range(COLS // 128))
    sums = jnp.sum(lanes.T, axis=0, keepdims=True)
    for i in range(TOK // 128):
        squares_ref[:, i : i + 1, :] = jnp.broadcast_to(
            sums[:, i * 128 : (i + 1) * 128][None], (NZ, 1, 128)
        )


def product(z, base, weight, context):
    return pl.pallas_call(
        kernel,
        out_shape=[
            jax.ShapeDtypeStruct((TOK, COLS), jnp.bfloat16),
            jax.ShapeDtypeStruct((NZ, TOK // 128, 128), jnp.float32),
        ],
        in_specs=[pl.BlockSpec(memory_space=pltpu.SMEM)]
        + [pl.BlockSpec(memory_space=pltpu.HBM)] * 3,
        out_specs=[pl.BlockSpec(memory_space=pltpu.VMEM)] * 2,
        scratch_shapes=[
            pltpu.VMEM((TOK, COLS), jnp.bfloat16),
            pltpu.VMEM((4, 1024, COLS), jnp.bfloat16),
            pltpu.VMEM((4, 4, TOK, FEAT), jnp.bfloat16),
            pltpu.SemaphoreType.DMA((9,)),
        ],
        compiler_params=pltpu.CompilerParams(vmem_limit_bytes=60 * 1024 * 1024),
        cost_estimate=pl.CostEstimate(
            flops=2 * TOK * COLS * H,
            bytes_accessed=(TOK + COLS) * H * 2 + TOK * COLS * 4,
            transcendentals=0,
        ),
    )(z, base, weight, context)


def shards(context, residual, policy_weight, master_weight, norm_gain):
    new_master = mix_rate * policy_weight.astype(jnp.float32) + (1.0 - mix_rate) * master_weight
    recast = new_master.astype(jnp.bfloat16)

    z = (lax.axis_index("tx") * 4 + lax.axis_index("ty")).astype(jnp.int32)
    f = lax.axis_index("fsdp")
    x, y, c = f // 8, (f // 2) % 4, f % 2

    gathered = lax.all_gather(context, Z, axis=0)
    piece = recast
    for pairs in (SPREAD, LIFT, LIFT_ON):
        piece = lax.ppermute(piece, ALL, pairs)

    row = jnp.zeros((4, 64, 1024), jnp.bfloat16)
    for dx in range(4):
        got = piece if dx == 0 else lax.ppermute(piece, "fsdp", partner(dx, 0, 0))
        row = lax.dynamic_update_slice(row, got[None], (x ^ dx, 0, 0))
    near = lax.ppermute(row, "fsdp", partner(0, 1, 0))
    back = lax.ppermute(row, "fsdp", partner(0, 3, 0))
    low = lax.ppermute(back[:2], "fsdp", partner(0, 1, 0))
    high = lax.ppermute(near[2:], "fsdp", partner(0, 3, 0))
    plane = jnp.zeros((16, 64, 1024), jnp.bfloat16)
    for got, dy, at in ((row, 0, 0), (near, 1, 0), (back, 3, 0), (low, 2, 0), (high, 2, 2)):
        plane = lax.dynamic_update_slice(plane, got, ((y ^ dy) * 4 + at, 0, 0))
    other = lax.ppermute(plane, "fsdp", partner(0, 0, 1))
    pieces = jnp.zeros((32, 64, 1024), jnp.bfloat16)
    pieces = lax.dynamic_update_slice(pieces, plane, (c * 16, 0, 0))
    pieces = lax.dynamic_update_slice(pieces, other, ((1 - c) * 16, 0, 0))
    weight = pieces.reshape(4, COLS, 1024).transpose(0, 2, 1)
    hidden, squares = product(z[None], residual, weight, gathered)

    totals = jnp.sum(lax.all_to_all(squares, Z, 0, 0, tiled=True), axis=0)
    square_mean = (totals.reshape(TOK) / D)[:, None]
    normed = (
        hidden * lax.rsqrt(square_mean + 1e-05) * norm_gain.astype(jnp.float32)[None, :]
    ).astype(jnp.bfloat16)
    return (normed, new_master)


def solution(mesh):
    return jax.shard_map(
        shards,
        mesh=mesh,
        in_specs=(
            P("fsdp", ("tx", "ty")),
            P("fsdp", ("ty", "tx")),
            P(("ty", "fsdp"), "tx"),
            P(("ty", "fsdp"), "tx"),
            P(("ty", "tx")),
        ),
        out_specs=(P("fsdp", ("ty", "tx")), P(("ty", "fsdp"), "tx")),
        check_vma=False,
    )
```

```python
import jax
import jax.numpy as jnp
from jax import lax
from jax.experimental import pallas as pl
from jax.experimental.pallas import tpu as pltpu
from jax.sharding import PartitionSpec as P

D = 8192
H = 4096
Z = ("tx", "ty")
ALL = ("fsdp", "tx", "ty")
NZ = 16

mix_rate = 0.6

TOK = 1024
FEAT = 256
COLS = 512


def place(f, t, y):
    return (f * 4 + t) * 4 + y


def column(r, turn):
    return ((r % 4) * 4 + (turn % 2) * 2 + r // 4) * 2 + turn // 2


SPREAD = []
LIFT = []
LIFT_ON = []
for y in range(4):
    for u in range(4):
        for r in range(8):
            for t in range(4):
                there = column(r, (u - t + y) % 4)
                SPREAD.append((place(8 * u + r, t, y), place(there, t, y)))
                step = (0, 1, 1 - 2 * (there % 2), -1)[(u - t) % 4]
                middle = (t + step) % 4
                LIFT.append((place(there, t, y), place(there, middle, y)))
                LIFT_ON.append((place(there, middle, y), place(there, u, y)))


def partner(dx, dy, dc):
    pairs = []
    for x in range(4):
        for y in range(4):
            for c in range(2):
                pairs.append(((x * 4 + y) * 2 + c, ((x ^ dx) * 4 + (y ^ dy)) * 2 + (c ^ dc)))
    return pairs


def kernel(z_ref, base_hbm, weight_hbm, context_hbm, out_ref, squares_ref, base, weight, context, sems):
    first = z_ref[0] // 4 + z_ref[0] % 4
    copies = []
    for turn in range(4):
        for half in range(2):
            plane = pl.ds((first - turn + 4) % 4 * 4 + 2 * half, 2)
            rows = pl.ds(512 * half, 512)
            k = 4 * turn + 2 * half
            copies.append(
                (
                    pltpu.make_async_copy(
                        weight_hbm.at[turn, rows], weight.at[turn, rows], sems.at[k]
                    ),
                    pltpu.make_async_copy(
                        context_hbm.at[plane], context.at[turn, pl.ds(2 * half, 2)], sems.at[k + 1]
                    ),
                )
            )
    base_copy = pltpu.make_async_copy(base_hbm, base, sems.at[16])
    for pair in copies:
        pair[0].start()
        pair[1].start()
    base_copy.start()
    total = 0
    for chunk, pair in enumerate(copies):
        turn, half = chunk // 2, chunk % 2
        pair[0].wait()
        pair[1].wait()
        block = jnp.concatenate([context[turn, 2 * half + i] for i in range(2)], axis=1)
        total += jnp.dot(
            block,
            weight[turn, 512 * half : 512 * (half + 1)],
            preferred_element_type=jnp.float32,
        )
    base_copy.wait()
    total += base[...].astype(jnp.float32)
    out_ref[...] = total.astype(jnp.bfloat16)
    squared = total * total
    lanes = sum(squared[:, i * 128 : (i + 1) * 128] for i in range(COLS // 128))
    sums = jnp.sum(lanes.T, axis=0, keepdims=True)
    for i in range(TOK // 128):
        squares_ref[:, i : i + 1, :] = jnp.broadcast_to(
            sums[:, i * 128 : (i + 1) * 128][None], (NZ, 1, 128)
        )


def product(z, base, weight, context):
    return pl.pallas_call(
        kernel,
        out_shape=[
            jax.ShapeDtypeStruct((TOK, COLS), jnp.bfloat16),
            jax.ShapeDtypeStruct((NZ, TOK // 128, 128), jnp.float32),
        ],
        in_specs=[pl.BlockSpec(memory_space=pltpu.SMEM)]
        + [pl.BlockSpec(memory_space=pltpu.HBM)] * 3,
        out_specs=[pl.BlockSpec(memory_space=pltpu.VMEM)] * 2,
        scratch_shapes=[
            pltpu.VMEM((TOK, COLS), jnp.bfloat16),
            pltpu.VMEM((4, 1024, COLS), jnp.bfloat16),
            pltpu.VMEM((4, 4, TOK, FEAT), jnp.bfloat16),
            pltpu.SemaphoreType.DMA((17,)),
        ],
        compiler_params=pltpu.CompilerParams(vmem_limit_bytes=50 * 1024 * 1024),
        cost_estimate=pl.CostEstimate(
            flops=2 * TOK * COLS * H,
            bytes_accessed=(TOK + COLS) * H * 2 + TOK * COLS * 4,
            transcendentals=0,
        ),
    )(z, base, weight, context)


def shards(context, residual, policy_weight, master_weight, norm_gain):
    new_master = mix_rate * policy_weight.astype(jnp.float32) + (1.0 - mix_rate) * master_weight
    recast = new_master.astype(jnp.bfloat16)

    z = (lax.axis_index("tx") * 4 + lax.axis_index("ty")).astype(jnp.int32)
    f = lax.axis_index("fsdp")
    x, y, c = f // 8, (f // 2) % 4, f % 2

    gathered = lax.all_gather(context, Z, axis=0)
    piece = recast
    for pairs in (SPREAD, LIFT, LIFT_ON):
        piece = lax.ppermute(piece, ALL, pairs)

    row = jnp.zeros((4, 64, 1024), jnp.bfloat16)
    for dx in range(4):
        got = piece if dx == 0 else lax.ppermute(piece, "fsdp", partner(dx, 0, 0))
        row = lax.dynamic_update_slice(row, got[None], (x ^ dx, 0, 0))
    near = lax.ppermute(row, "fsdp", partner(0, 1, 0))
    back = lax.ppermute(row, "fsdp", partner(0, 3, 0))
    low = lax.ppermute(back[:2], "fsdp", partner(0, 1, 0))
    high = lax.ppermute(near[2:], "fsdp", partner(0, 3, 0))
    plane = jnp.zeros((16, 64, 1024), jnp.bfloat16)
    for got, dy, at in ((row, 0, 0), (near, 1, 0), (back, 3, 0), (low, 2, 0), (high, 2, 2)):
        plane = lax.dynamic_update_slice(plane, got, ((y ^ dy) * 4 + at, 0, 0))
    other = lax.ppermute(plane, "fsdp", partner(0, 0, 1))
    pieces = jnp.zeros((32, 64, 1024), jnp.bfloat16)
    pieces = lax.dynamic_update_slice(pieces, plane, (c * 16, 0, 0))
    pieces = lax.dynamic_update_slice(pieces, other, ((1 - c) * 16, 0, 0))
    weight = pieces.reshape(4, COLS, 1024).transpose(0, 2, 1)
    hidden, squares = product(z[None], residual, weight, gathered)

    totals = jnp.sum(lax.all_to_all(squares, Z, 0, 0, tiled=True), axis=0)
    square_mean = (totals.reshape(TOK) / D)[:, None]
    normed = (
        hidden * lax.rsqrt(square_mean + 1e-05) * norm_gain.astype(jnp.float32)[None, :]
    ).astype(jnp.bfloat16)
    return (normed, new_master)


def solution(mesh):
    return jax.shard_map(
        shards,
        mesh=mesh,
        in_specs=(
            P("fsdp", ("tx", "ty")),
            P("fsdp", ("ty", "tx")),
            P(("ty", "fsdp"), "tx"),
            P(("ty", "fsdp"), "tx"),
            P(("ty", "tx")),
        ),
        out_specs=(P("fsdp", ("ty", "tx")), P(("ty", "fsdp"), "tx")),
        check_vma=False,
    )
```

```python
import jax
import jax.numpy as jnp
from jax import lax
from jax.experimental import pallas as pl
from jax.experimental.pallas import tpu as pltpu
from jax.sharding import PartitionSpec as P

D = 8192
H = 4096
Z = ("tx", "ty")
ALL = ("fsdp", "tx", "ty")
NZ = 16

mix_rate = 0.6

TOK = 1024
FEAT = 256
COLS = 512


def place(f, t, y):
    return (f * 4 + t) * 4 + y


def column(r, turn):
    return ((r % 4) * 4 + (turn % 2) * 2 + r // 4) * 2 + turn // 2


SPREAD = []
LIFT = []
LIFT_ON = []
for y in range(4):
    for u in range(4):
        for r in range(8):
            for t in range(4):
                there = column(r, (u - t + y) % 4)
                SPREAD.append((place(8 * u + r, t, y), place(there, t, y)))
                step = (0, 1, 1 - 2 * (there % 2), -1)[(u - t) % 4]
                middle = (t + step) % 4
                LIFT.append((place(there, t, y), place(there, middle, y)))
                LIFT_ON.append((place(there, middle, y), place(there, u, y)))


def partner(dx, dy, dc):
    pairs = []
    for x in range(4):
        for y in range(4):
            for c in range(2):
                pairs.append(((x * 4 + y) * 2 + c, ((x ^ dx) * 4 + (y ^ dy)) * 2 + (c ^ dc)))
    return pairs


def kernel(z_ref, base, weight_hbm, context_hbm, out_ref, squares_ref, weight, context, sems):
    first = z_ref[0] // 4 + z_ref[0] % 4
    copies = []
    for turn in range(4):
        for half in range(2):
            plane = pl.ds((first - turn + 4) % 4 * 4 + 2 * half, 2)
            rows = pl.ds(512 * half, 512)
            k = 4 * turn + 2 * half
            copies.append(
                (
                    pltpu.make_async_copy(
                        weight_hbm.at[turn, rows], weight.at[turn, rows], sems.at[k]
                    ),
                    pltpu.make_async_copy(
                        context_hbm.at[plane], context.at[turn, pl.ds(2 * half, 2)], sems.at[k + 1]
                    ),
                )
            )
    for pair in copies:
        pair[0].start()
        pair[1].start()
    total = 0
    for chunk, pair in enumerate(copies):
        turn, half = chunk // 2, chunk % 2
        pair[0].wait()
        pair[1].wait()
        block = jnp.concatenate([context[turn, 2 * half + i] for i in range(2)], axis=1)
        total += jnp.dot(
            block,
            weight[turn, 512 * half : 512 * (half + 1)],
            preferred_element_type=jnp.float32,
        )
    total += base[...].astype(jnp.float32)
    out_ref[...] = total.astype(jnp.bfloat16)
    squared = total * total
    lanes = sum(squared[:, i * 128 : (i + 1) * 128] for i in range(COLS // 128))
    sums = jnp.sum(lanes.T, axis=0, keepdims=True)
    for i in range(TOK // 128):
        squares_ref[:, i : i + 1, :] = jnp.broadcast_to(
            sums[:, i * 128 : (i + 1) * 128][None], (NZ, 1, 128)
        )


def product(z, base, weight, context):
    return pl.pallas_call(
        kernel,
        out_shape=[
            jax.ShapeDtypeStruct((TOK, COLS), jnp.bfloat16),
            jax.ShapeDtypeStruct((NZ, TOK // 128, 128), jnp.float32),
        ],
        in_specs=[pl.BlockSpec(memory_space=pltpu.SMEM)]
        + [pl.BlockSpec(memory_space=pltpu.VMEM)]
        + [pl.BlockSpec(memory_space=pltpu.HBM)] * 2,
        out_specs=[pl.BlockSpec(memory_space=pltpu.VMEM)] * 2,
        scratch_shapes=[
            pltpu.VMEM((4, 1024, COLS), jnp.bfloat16),
            pltpu.VMEM((4, 4, TOK, FEAT), jnp.bfloat16),
            pltpu.SemaphoreType.DMA((16,)),
        ],
        compiler_params=pltpu.CompilerParams(vmem_limit_bytes=50 * 1024 * 1024),
        cost_estimate=pl.CostEstimate(
            flops=2 * TOK * COLS * H,
            bytes_accessed=(TOK + COLS) * H * 2 + TOK * COLS * 4,
            transcendentals=0,
        ),
    )(z, base, weight, context)


def shards(context, residual, policy_weight, master_weight, norm_gain):
    new_master = mix_rate * policy_weight.astype(jnp.float32) + (1.0 - mix_rate) * master_weight
    recast = new_master.astype(jnp.bfloat16)

    z = (lax.axis_index("tx") * 4 + lax.axis_index("ty")).astype(jnp.int32)
    f = lax.axis_index("fsdp")
    x, y, c = f // 8, (f // 2) % 4, f % 2

    gathered = lax.all_gather(context, Z, axis=0)
    piece = recast
    for pairs in (SPREAD, LIFT, LIFT_ON):
        piece = lax.ppermute(piece, ALL, pairs)

    row = jnp.zeros((4, 64, 1024), jnp.bfloat16)
    for dx in range(4):
        got = piece if dx == 0 else lax.ppermute(piece, "fsdp", partner(dx, 0, 0))
        row = lax.dynamic_update_slice(row, got[None], (x ^ dx, 0, 0))
    near = lax.ppermute(row, "fsdp", partner(0, 1, 0))
    back = lax.ppermute(row, "fsdp", partner(0, 3, 0))
    low = lax.ppermute(back[:2], "fsdp", partner(0, 1, 0))
    high = lax.ppermute(near[2:], "fsdp", partner(0, 3, 0))
    plane = jnp.zeros((16, 64, 1024), jnp.bfloat16)
    for got, dy, at in ((row, 0, 0), (near, 1, 0), (back, 3, 0), (low, 2, 0), (high, 2, 2)):
        plane = lax.dynamic_update_slice(plane, got, ((y ^ dy) * 4 + at, 0, 0))
    other = lax.ppermute(plane, "fsdp", partner(0, 0, 1))
    pieces = jnp.zeros((32, 64, 1024), jnp.bfloat16)
    pieces = lax.dynamic_update_slice(pieces, plane, (c * 16, 0, 0))
    pieces = lax.dynamic_update_slice(pieces, other, ((1 - c) * 16, 0, 0))
    weight = pieces.reshape(4, COLS, 1024).transpose(0, 2, 1)
    hidden, squares = product(z[None], residual, weight, gathered)

    totals = jnp.sum(lax.all_to_all(squares, Z, 0, 0, tiled=True), axis=0)
    square_mean = (totals.reshape(TOK) / D)[:, None]
    normed = (
        hidden * lax.rsqrt(square_mean + 1e-05) * norm_gain.astype(jnp.float32)[None, :]
    ).astype(jnp.bfloat16)
    return (normed, new_master)


def solution(mesh):
    return jax.shard_map(
        shards,
        mesh=mesh,
        in_specs=(
            P("fsdp", ("tx", "ty")),
            P("fsdp", ("ty", "tx")),
            P(("ty", "fsdp"), "tx"),
            P(("ty", "fsdp"), "tx"),
            P(("ty", "tx")),
        ),
        out_specs=(P("fsdp", ("ty", "tx")), P(("ty", "fsdp"), "tx")),
        check_vma=False,
    )
```
